128 devices in a mesh: ctx: 32 (over y, x, core), head: 4 (over z).
Axes of the slice: x: 4, y: 4, z: 4, core: 2. Of those that a mesh axis runs over, the one named last changes fastest.
Arguments:
- queries: bfloat16 [192, 8192], P('ctx', 'head'), may hold values from -14 to 14
- keys: bfloat16 [262144, 1024], P('ctx', 'head'), may hold values from -8 to 8
- values: bfloat16 [262144, 1024], P('ctx', 'head'), may hold values from -6 to 6
- lengths: int32 [32], P('ctx'), may hold values from 1 to 8192, as said below
Outputs:
- mixed: bfloat16 [192, 8192], P('ctx')
- log_norm: float32 [192, 64], P('ctx')
The draws below stay inside these ranges and needn't reach their ends.
Inputs may be any that keep to these rules, and one draw needn't show every extreme that they name: `lengths`: block 0 is always full; the last block holds at most 4096 valid tokens; every other block at least 4096.
All inputs are finite; a program needn't handle non-finite values.
Results may differ from the reference program's by a relative error of at most 0.0033.
Values may be sent and summed in bfloat16 or wider, within the bound.
No kernel may reach another device: no remote copies, remote signals or barrier semaphores. Data moves between devices by JAX's collectives and lax.ppermute only.
A program may use at most 256 MiB of HBM per device.

```python
import math
import jax
import jax.numpy as jnp
from jax import lax

HQ = 64
KVH = 8
DH = 128
QT = 192
BLOCK = 8192
TILE = 1024
NBLK = 32
CONTEXT = 262144


def draw_queries(key, part):
    key = jax.random.fold_in(key, 1)
    drawn = jnp.clip(3.5 * jax.random.normal(key, (QT, HQ, DH), jnp.float32), -14.0, 14.0)
    return drawn.reshape(QT, HQ * DH).astype(jnp.bfloat16)


def draw_keys(key, part):
    key = jax.random.fold_in(key, 2)
    drawn = jnp.clip(jax.random.normal(key, (CONTEXT, KVH * DH), jnp.float32), -5.0, 5.0)
    return drawn.astype(jnp.bfloat16)


def draw_lengths(key, part):
    key = jax.random.fold_in(key, 3)
    block_counts = jax.random.randint(key, (NBLK,), BLOCK // 2, BLOCK + 1, jnp.int32)
    block_counts = block_counts.at[0].set(BLOCK)
    final_count = jax.random.randint(jax.random.fold_in(key, 1), (), 1, BLOCK // 2 + 1, jnp.int32)
    return block_counts.at[NBLK - 1].set(final_count)


def block_levels(own_key, extent, cuts, low, high):
    level, own = 1.0, jax.random.fold_in(own_key, 6)
    for position, shards_of in cuts:
        draws = jnp.exp(jax.random.uniform(jax.random.fold_in(own, position), (shards_of,), jnp.float32, low / len(cuts), high / len(cuts)))
        level = level * jnp.repeat(draws, extent[position] // shards_of).reshape([-1 if axis == position else 1 for axis in range(len(extent))])
    return level


def centred(own_key, dims, width, most, pieces=(), kind=jnp.bfloat16):
    factor_of = block_levels(own_key, dims, pieces, -0.22, 0.18) if pieces else 1.0
    result = jax.random.normal(own_key, dims, jnp.float32) * width * factor_of
    return jnp.minimum(jnp.maximum(result, -most), most).astype(kind)


def setup_inputs(seed: int = 0) -> dict:
    key_list = jax.random.split(jax.random.key(seed), 5)
    return {
        "queries": draw_queries(jax.random.fold_in(key_list[4], 71), 0),
        "keys": draw_keys(jax.random.fold_in(key_list[4], 71), 0),
        "values": centred(key_list[2], (CONTEXT, KVH * DH), 1.0, 6.0, ((0, 32), (1, 4))),
        "lengths": draw_lengths(jax.random.fold_in(key_list[4], 71), 0),
    }


masked_score = -1e+30

def reference(queries, keys, values, lengths):
    group_size = HQ // KVH
    query_four = queries.astype(jnp.float32).reshape(QT, KVH, group_size, DH)
    score_scale = 1.0 / math.sqrt(DH)
    per_block = BLOCK // TILE

    def one_tile(state, tile_index):
        peak_run, numer_run, denom_run = state
        first_key = tile_index * TILE
        key_tile = lax.dynamic_slice_in_dim(keys, first_key, TILE, 0).astype(jnp.float32).reshape(TILE, KVH, DH)
        value_tile = lax.dynamic_slice_in_dim(values, first_key, TILE, 0).astype(jnp.float32).reshape(TILE, KVH, DH)
        limit = lengths[tile_index // per_block] - tile_index % per_block * TILE
        scores = jnp.einsum('qkgd,ckd->qkgc', query_four, key_tile) * score_scale
        is_valid = jnp.arange(TILE, dtype=jnp.int32) < limit
        scores = jnp.where(is_valid, scores, masked_score)
        tile_peak = lax.optimization_barrier(jnp.max(scores, axis=-1))
        weights = jnp.exp(scores - tile_peak[..., None])
        tile_total = lax.optimization_barrier(jnp.sum(weights, axis=-1))
        tile_probs = lax.optimization_barrier(weights.astype(jnp.bfloat16)).astype(jnp.float32)
        tile_out = jnp.einsum('qkgc,ckd->qkgd', tile_probs, value_tile)
        new_peak = jnp.maximum(peak_run, tile_peak)
        old_weight = jnp.exp(peak_run - new_peak)
        new_weight = jnp.exp(tile_peak - new_peak)
        numer_run = numer_run * old_weight[..., None] + tile_out * new_weight[..., None]
        denom_run = denom_run * old_weight + tile_total * new_weight
        return ((new_peak, numer_run, denom_run), None)
    initial = (jnp.full((QT, KVH, group_size), -jnp.inf, jnp.float32), jnp.zeros((QT, KVH, group_size, DH), jnp.float32), jnp.zeros((QT, KVH, group_size), jnp.float32))
    tile_ids = jnp.arange(NBLK * BLOCK // TILE, dtype=jnp.int32)
    final_state, unused = lax.scan(one_tile, initial, tile_ids)
    peak_all, numer_all, denom_all = final_state
    mixed = (numer_all / denom_all[..., None]).reshape(QT, HQ * DH).astype(jnp.bfloat16)
    log_norm = (peak_all + jnp.log(denom_all)).reshape(QT, HQ)
    return (mixed, log_norm)
```

```python
import math

import jax
import jax.numpy as jnp
from jax import lax
from jax.experimental import pallas as pl
from jax.experimental.pallas import tpu as pltpu
from jax.sharding import PartitionSpec as P

DH = 128
f32, bf16 = jnp.float32, jnp.bfloat16
LOG2E = 1.4426950408889634
LN2 = 0.6931471805599453
TO_LOG2 = LOG2E / math.sqrt(DH)

CHIPS, CORES = 16, 2
TOK, GRP, KV = 6, 8, 2
ROWS = TOK * GRP
HALF = CHIPS * ROWS
COLS = CORES * HALF
CTX = 8192
CHUNK = 2048
PROBE = 256
LROW, MROW, AUG = DH, DH + 8, DH + 16
MSG = KV * ROWS + 8

VMEM = pl.BlockSpec(memory_space=pltpu.VMEM)
SMEM = pl.BlockSpec(memory_space=pltpu.SMEM)
ANY = pl.BlockSpec(memory_space=pl.ANY)
PARAMS = pltpu.CompilerParams(vmem_limit_bytes=60 * 2**20)


def spread_body(q_ref, out_ref):
    q = q_ref[...].astype(f32)
    rows = jnp.concatenate([q[:, i * DH : (i + 1) * DH] for i in range(KV * GRP)], axis=0)
    out_ref[...] = jnp.broadcast_to(rows.astype(bf16)[None], out_ref.shape)


def attend_body(
    len_ref, q_own, q_other, k_hbm, v_hbm, own_ref, other_ref, kbuf, vbuf, qt, vt, peak, ksem, vsem
):
    chunks = CTX // CHUNK
    outs = (own_ref, other_ref)

    def k_copy(c):
        part = pl.ds(c * CHUNK, CHUNK)
        return pltpu.make_async_copy(k_hbm.at[part], kbuf.at[part], ksem.at[c])

    def v_copy(c):
        part = pl.ds(c * CHUNK, CHUNK)
        return pltpu.make_async_copy(v_hbm.at[part], vbuf.at[part], vsem.at[c])

    for c in range(chunks):
        k_copy(c).start()
        v_copy(c).start()
    valid = len_ref[0]
    for h in range(KV):
        for i, src in enumerate((q_own, q_other)):
            x = src[:, h * ROWS : (h + 1) * ROWS, :].reshape(HALF, DH)
            qt[h, :, i * HALF : (i + 1) * HALF] = x.astype(f32).T.astype(bf16)
    k_copy(0).wait()
    v_copy(0).wait()

    for h in range(KV):
        s = jnp.dot(kbuf[0:PROBE, h * DH : (h + 1) * DH], qt[h], preferred_element_type=f32)
        pos = lax.broadcasted_iota(jnp.int32, (PROBE, 1), 0)
        s = jnp.where(pos < valid, s, -1e30)
        peak[h] = jnp.max(s, axis=0, keepdims=True) * TO_LOG2

    def turn_values(h, first, size):
        ok = lax.broadcasted_iota(jnp.int32, (1, size), 1) + first < valid
        v = vbuf[pl.ds(first, size), h * DH : (h + 1) * DH].astype(f32).T
        vt[0:DH, 0:size] = jnp.where(ok, v, 0.0).astype(bf16)
        ones = jnp.broadcast_to(jnp.where(ok, 1.0, 0.0), (AUG - DH, size))
        vt[DH:AUG, 0:size] = ones.astype(bf16)

    def chunk(c, h, fresh):
        first = pl.multiple_of(c * CHUNK, CHUNK)
        turn_values(h, first, CHUNK)
        k = kbuf[pl.ds(first, CHUNK), h * DH : (h + 1) * DH]
        for i, out in enumerate(outs):
            part = slice(i * HALF, (i + 1) * HALF)
            s = jnp.dot(k, qt[h, :, part], preferred_element_type=f32)
            p = jnp.exp2(jnp.minimum(s * TO_LOG2 - peak[h, :, part], 100.0)).astype(bf16)
            pv = jnp.dot(vt[...], p, preferred_element_type=f32)
            if fresh:
                out[h] = pv
            else:
                out[h] += pv

    for h in range(KV):
        chunk(0, h, True)

    def later(c, carry):
        k_copy(c).wait()
        v_copy(c).wait()

        @pl.when(c * CHUNK < valid)
        def _():
            for h in range(KV):
                chunk(c, h, False)

        return carry

    lax.fori_loop(1, chunks, later, 0)

    low = jnp.minimum(jnp.min(own_ref[:, LROW, :]), jnp.min(other_ref[:, LROW, :]))
    high = jnp.maximum(jnp.max(own_ref[:, LROW, :]), jnp.max(other_ref[:, LROW, :]))

    @pl.when(jnp.logical_not((low > 0.25) & (high < 2.0**60)))
    def _():
        size = 512

        def part_scores(h, i, first):
            k = kbuf[pl.ds(first, size), h * DH : (h + 1) * DH]
            s = jnp.dot(k, qt[h, :, i * HALF : (i + 1) * HALF], preferred_element_type=f32)
            pos = lax.broadcasted_iota(jnp.int32, (size, 1), 0) + first
            return jnp.where(pos < valid, s * TO_LOG2, -1e30)

        for h in range(KV):
            for i, out in enumerate(outs):
                part = slice(i * HALF, (i + 1) * HALF)

                def top(c, best):
                    s = part_scores(h, i, pl.multiple_of(c * size, size))
                    return jnp.maximum(best, jnp.max(s, axis=0, keepdims=True))

                peak[h, :, part] = lax.fori_loop(
                    0, CTX // size, top, jnp.full((1, HALF), -1e30, f32)
                )
                out[h] = jnp.zeros((AUG, HALF), f32)

                def add(c, carry):
                    first = pl.multiple_of(c * size, size)
                    turn_values(h, first, size)
                    p = jnp.exp2(part_scores(h, i, first) - peak[h, :, part]).astype(bf16)
                    out[h] += jnp.dot(vt[:, 0:size], p, preferred_element_type=f32)
                    return carry

                lax.fori_loop(0, CTX // size, add, 0)

    for h in range(KV):
        for i, out in enumerate(outs):
            part = slice(i * HALF, (i + 1) * HALF)
            out[h, MROW:AUG, :] = jnp.broadcast_to(peak[h, :, part], (AUG - MROW, HALF))


def pair_body(a_ref, b_ref, out_ref):
    for h in range(KV):
        ma, mb = a_ref[h, MROW : MROW + 1, :], b_ref[h, MROW : MROW + 1, :]
        top = jnp.maximum(ma, mb)
        wa, wb = jnp.exp2(ma - top), jnp.exp2(mb - top)
        total = wa * a_ref[h, LROW : LROW + 1, :] + wb * b_ref[h, LROW : LROW + 1, :]
        num = a_ref[h, 0:DH, :] * (wa / total) + b_ref[h, 0:DH, :] * (wb / total)
        out_ref[:, h * ROWS : (h + 1) * ROWS, :] = num.T.reshape(CHIPS, ROWS, DH)
        norm = top + jnp.log2(total)
        for c in range(CHIPS):
            out_ref[c, KV * ROWS : KV * ROWS + 1, h * ROWS : (h + 1) * ROWS] = norm[
                :, c * ROWS : (c + 1) * ROWS
            ]


def merge_body(in_ref, out_ref):
    rows = KV * ROWS
    norm = in_ref[:, rows, :]
    norm = jnp.where(lax.broadcasted_iota(jnp.int32, norm.shape, 1) < rows, norm, 0.0)
    top = jnp.max(norm, axis=0, keepdims=True)
    w = jnp.exp2(norm - top)
    total = jnp.sum(w, axis=0, keepdims=True)
    w = (w / total).T
    o = in_ref[0, 0:rows, :] * w[0:rows, 0:1]
    for c in range(1, CHIPS):
        o = o + in_ref[c, 0:rows, :] * w[0:rows, c : c + 1]
    out_ref[:, 0:rows, :] = jnp.broadcast_to(o[None], (out_ref.shape[0], rows, DH))
    norm = (top + jnp.log2(total)) * LN2
    out_ref[:, rows:MSG, :] = jnp.broadcast_to(norm[None], (out_ref.shape[0], MSG - rows, DH))


def finish_body(in_ref, mixed_ref, norm_ref):
    rows, heads = KV * ROWS, KV * GRP
    parts = in_ref.shape[0]
    token = lax.broadcasted_iota(jnp.int32, (8, DH), 0)
    lane = lax.broadcasted_iota(jnp.int32, (8, DH), 1)
    lane_of = lax.broadcasted_iota(jnp.int32, (DH, parts * heads), 0)
    head_of = lax.broadcasted_iota(jnp.int32, (DH, parts * heads), 1)
    norm = jnp.zeros((8, parts * heads), f32)
    for z in range(parts):
        o = in_ref[z, 0:rows, :].astype(bf16).astype(f32)
        for i in range(heads):
            mixed_ref[:, (z * heads + i) * DH : (z * heads + i + 1) * DH] = o[
                i * TOK : (i + 1) * TOK, :
            ].astype(bf16)
        mine = jnp.where((lane % TOK == token) & (lane < rows), in_ref[z, rows : rows + 1, :], 0.0)
        pick = jnp.where(lane_of // TOK + z * heads == head_of, 1.0, 0.0)
        pick = jnp.where(lane_of < rows, pick, 0.0)
        norm = norm + jnp.dot(
            mine, pick, preferred_element_type=f32, precision=lax.Precision.HIGHEST
        )
    norm_ref[...] = norm[0:TOK, :]


def call(body, out_shape, in_specs, scratch=()):
    many = isinstance(out_shape, tuple)
    return pl.pallas_call(
        body,
        out_shape=out_shape,
        in_specs=in_specs,
        out_specs=(VMEM,) * len(out_shape) if many else VMEM,
        scratch_shapes=list(scratch),
        compiler_params=PARAMS,
    )


def on_device(queries, keys, values, lengths):
    shape = jax.ShapeDtypeStruct
    same_core = [[2 * i + c for i in range(CHIPS)] for c in range(CORES)]
    swap = [(i, i ^ 1) for i in range(CHIPS * CORES)]
    parts = lax.axis_size("head")

    sent = call(spread_body, shape((CHIPS, KV * ROWS, DH), bf16), [VMEM])(queries)
    q_own = lax.all_to_all(sent, "ctx", 0, 0, tiled=True, axis_index_groups=same_core)
    q_other = lax.ppermute(q_own, "ctx", swap)
    acc = shape((KV, AUG, HALF), f32)
    own, other = call(
        attend_body,
        (acc, acc),
        [SMEM, VMEM, VMEM, ANY, ANY],
        [
            pltpu.VMEM((CTX, KV * DH), bf16),
            pltpu.VMEM((CTX, KV * DH), bf16),
            pltpu.VMEM((KV, DH, COLS), bf16),
            pltpu.VMEM((AUG, CHUNK), bf16),
            pltpu.VMEM((KV, 1, COLS), f32),
            pltpu.SemaphoreType.DMA((CTX // CHUNK,)),
            pltpu.SemaphoreType.DMA((CTX // CHUNK,)),
        ],
    )(lengths, q_own, q_other, keys, values)
    partner = lax.ppermute(other, "ctx", swap)
    sent = call(pair_body, shape((CHIPS, MSG, DH), f32), [VMEM, VMEM])(own, partner)
    got = lax.all_to_all(sent, "ctx", 0, 0, tiled=True, axis_index_groups=same_core)
    sent = call(merge_body, shape((parts, MSG, DH), f32), [VMEM])(got)
    got = lax.all_to_all(sent, "head", 0, 0, tiled=True)
    heads = parts * KV * GRP
    return call(finish_body, (shape((TOK, heads * DH), bf16), shape((TOK, heads), f32)), [VMEM])(
        got
    )


def solution(mesh):
    return jax.shard_map(
        on_device,
        mesh=mesh,
        in_specs=(P("ctx", "head"), P("ctx", "head"), P("ctx", "head"), P("ctx")),
        out_specs=(P("ctx", None), P("ctx", None)),
        check_vma=False,
    )
```

```python
import math

import jax
import jax.numpy as jnp
from jax import lax
from jax.experimental import pallas as pl
from jax.experimental.pallas import tpu as pltpu
from jax.sharding import PartitionSpec as P

DH = 128
f32, bf16 = jnp.float32, jnp.bfloat16
LOG2E = 1.4426950408889634
LN2 = 0.6931471805599453
TO_LOG2 = LOG2E / math.sqrt(DH)

CHIPS, CORES = 16, 2
TOK, GRP, KV = 6, 8, 2
ROWS = TOK * GRP
HALF = CHIPS * ROWS
COLS = CORES * HALF
CTX = 8192
CHUNKS = (1024, 3072, 4096)
STARTS = (0, 1024, 4096)
LROW, MROW, AUG = DH, DH + 8, DH + 16
RIM = 16
MSG = KV * ROWS + RIM
STEPS = 32766.0

VMEM = pl.BlockSpec(memory_space=pltpu.VMEM)
SMEM = pl.BlockSpec(memory_space=pltpu.SMEM)
ANY = pl.BlockSpec(memory_space=pl.ANY)
SMALL, LARGE = 8, 48


def spread_body(q_ref, out_ref):
    q = q_ref[...].astype(f32)
    rows = jnp.concatenate([q[:, i * DH : (i + 1) * DH] for i in range(KV * GRP)], axis=0)
    out_ref[...] = jnp.broadcast_to(rows.astype(bf16)[None], out_ref.shape)


def attend_body(
    len_ref, q_own, q_other, k_hbm, v_hbm, own_ref, other_ref, kbuf, vbuf, qt, vt, ksem, vsem
):
    outs = (own_ref, other_ref)

    def copies(c):
        part = pl.ds(STARTS[c], CHUNKS[c])
        return (
            pltpu.make_async_copy(k_hbm.at[part], kbuf.at[part], ksem.at[c]),
            pltpu.make_async_copy(v_hbm.at[part], vbuf.at[part], vsem.at[c]),
        )

    for c in range(len(CHUNKS)):
        for copy in copies(c):
            copy.start()
    valid = len_ref[0]

    def turn_queries(h):
        for i, src in enumerate((q_own, q_other)):
            x = src[:, h * ROWS : (h + 1) * ROWS, :].reshape(HALF, DH).astype(f32).T * TO_LOG2
            high = x.astype(bf16)
            qt[h, 0:DH, i * HALF : (i + 1) * HALF] = high
            qt[h, DH : 2 * DH, i * HALF : (i + 1) * HALF] = (x - high.astype(f32)).astype(bf16)

    def turn_values(h, first, size):
        ok = lax.broadcasted_iota(jnp.int32, (1, size), 1) + first < valid
        v = vbuf[pl.ds(first, size), h * DH : (h + 1) * DH].astype(f32).T
        vt[0:DH, 0:size] = jnp.where(ok, v, 0.0).astype(bf16)
        ones = jnp.broadcast_to(jnp.where(ok, 1.0, 0.0), (AUG - DH, size))
        vt[DH:AUG, 0:size] = ones.astype(bf16)

    def scores(h, i, first, size):
        k = kbuf[pl.ds(first, size), h * DH : (h + 1) * DH]
        k = jnp.concatenate([k, k], axis=1)
        return jnp.dot(k, qt[h, :, i * HALF : (i + 1) * HALF], preferred_element_type=f32)

    def chunk(c, h):
        turn_values(h, STARTS[c], CHUNKS[c])
        for i, out in enumerate(outs):
            p = jnp.exp2(scores(h, i, STARTS[c], CHUNKS[c])).astype(bf16)
            pv = jnp.dot(vt[:, 0 : CHUNKS[c]], p, preferred_element_type=f32)
            if c == 0:
                out[h] = pv
            else:
                out[h] += pv

    turn_queries(0)
    for copy in copies(0):
        copy.wait()
    chunk(0, 0)
    turn_queries(1)
    chunk(0, 1)
    for c in range(1, len(CHUNKS)):
        for copy in copies(c):
            copy.wait()

        @pl.when(STARTS[c] < valid)
        def _():
            for h in range(KV):
                chunk(c, h)

    wrong = jnp.zeros((1, HALF), f32)
    for h in range(KV):
        for out in outs:
            total = out[h, LROW : LROW + 1, :]
            fine = (total > 2.0**-60) & (total < 2.0**90)
            wrong = wrong + jnp.where(fine, 0.0, 1.0)
            out[h, MROW:AUG, :] = jnp.zeros((AUG - MROW, HALF), f32)

    @pl.when(jnp.sum(wrong) > 0.5)
    def _():
        size = 512

        def masked(h, i, first):
            pos = lax.broadcasted_iota(jnp.int32, (size, 1), 0) + first
            return jnp.where(pos < valid, scores(h, i, first, size), -1e30)

        for h in range(KV):
            for i, out in enumerate(outs):

                def top(c, best):
                    s = masked(h, i, pl.multiple_of(c * size, size))
                    return jnp.maximum(best, jnp.max(s, axis=0, keepdims=True))

                start = jnp.full((1, HALF), -1e30, f32)
                peak = lax.fori_loop(0, CTX // size, top, start)
                out[h] = jnp.zeros((AUG, HALF), f32)

                def add(c, carry):
                    first = pl.multiple_of(c * size, size)
                    turn_values(h, first, size)
                    p = jnp.exp2(masked(h, i, first) - peak).astype(bf16)
                    out[h] += jnp.dot(vt[:, 0:size], p, preferred_element_type=f32)
                    return carry

                lax.fori_loop(0, CTX // size, add, 0)
                out[h, MROW:AUG, :] = jnp.broadcast_to(peak, (AUG - MROW, HALF))


def pair_body(a_ref, b_ref, out_ref):
    for h in range(KV):
        ma, mb = a_ref[h, MROW : MROW + 1, :], b_ref[h, MROW : MROW + 1, :]
        top = jnp.maximum(ma, mb)
        wa, wb = jnp.exp2(ma - top), jnp.exp2(mb - top)
        total = wa * a_ref[h, LROW : LROW + 1, :] + wb * b_ref[h, LROW : LROW + 1, :]
        num = a_ref[h, 0:DH, :] * (wa / total) + b_ref[h, 0:DH, :] * (wb / total)
        size = jnp.max(jnp.abs(num), axis=0, keepdims=True)
        power = jnp.ceil(jnp.log2(jnp.maximum(size * 1.0001, 2.0**-100)))
        num = num * (jnp.exp2(-power) * STEPS)
        norm = (top + jnp.log2(total)) * 16.0
        coarse = jnp.floor(norm)
        fine = jnp.floor((norm - coarse) * 32767.0)
        rim = jnp.concatenate([coarse, fine, power, jnp.zeros((RIM - 3, HALF), f32)], axis=0)
        rim = rim.astype(jnp.int32)
        codes = jnp.round(num.T).astype(jnp.int32).astype(jnp.int16)
        out_ref[:, h * ROWS : (h + 1) * ROWS, :] = codes.reshape(CHIPS, ROWS, DH)
        for c in range(CHIPS):
            out_ref[c, KV * ROWS : MSG, h * ROWS : (h + 1) * ROWS] = rim[
                :, c * ROWS : (c + 1) * ROWS
            ].astype(jnp.int16)


def merge_body(in_ref, out_ref):
    rows = KV * ROWS
    rim = in_ref[:, rows:MSG, :].astype(jnp.int32).astype(f32)
    used = lax.broadcasted_iota(jnp.int32, (CHIPS, DH), 1) < rows
    norm = jnp.where(used, rim[:, 0, :] * 0.0625 + rim[:, 1, :] * (0.0625 / 32767.0), 0.0)
    power = jnp.where(used, rim[:, 2, :], 0.0)
    top = jnp.max(norm, axis=0, keepdims=True)
    w = jnp.exp2(norm - top)
    total = jnp.sum(w, axis=0, keepdims=True)
    w = (w * jnp.exp2(power) / (total * STEPS)).T
    o = jnp.zeros((rows, DH), f32)
    for c in range(CHIPS):
        o = o + in_ref[c, 0:rows, :].astype(jnp.int32).astype(f32) * w[0:rows, c : c + 1]
    parts = out_ref.shape[0]
    out_ref[:, 0:rows, :] = jnp.broadcast_to(o.astype(bf16)[None], (parts, rows, DH))
    norm = (top + jnp.log2(total)) * LN2
    pieces = []
    for _ in range(3):
        piece = norm.astype(bf16).astype(f32)
        pieces.append(piece)
        norm = norm - piece
    rim = jnp.concatenate([*pieces, jnp.zeros((RIM - 3, DH), f32)], axis=0).astype(bf16)
    out_ref[:, rows:MSG, :] = jnp.broadcast_to(rim[None], (parts, RIM, DH))


def finish_body(in_ref, mixed_ref, norm_ref):
    rows, heads = KV * ROWS, KV * GRP
    parts = in_ref.shape[0]
    token = lax.broadcasted_iota(jnp.int32, (8, DH), 0)
    lane = lax.broadcasted_iota(jnp.int32, (8, DH), 1)
    lane_of = lax.broadcasted_iota(jnp.int32, (DH, parts * heads), 0)
    head_of = lax.broadcasted_iota(jnp.int32, (DH, parts * heads), 1)
    norm = jnp.zeros((8, parts * heads), f32)
    for z in range(parts):
        o = in_ref[z, 0:rows, :].astype(f32)
        for i in range(heads):
            mixed_ref[:, (z * heads + i) * DH : (z * heads + i + 1) * DH] = o[
                i * TOK : (i + 1) * TOK, :
            ].astype(bf16)
        rim = in_ref[z, rows:MSG, :].astype(f32)
        mine = jnp.where((lane % TOK == token) & (lane < rows), rim[0:1] + rim[1:2] + rim[2:3], 0.0)
        pick = jnp.where(lane_of // TOK + z * heads == head_of, 1.0, 0.0)
        pick = jnp.where(lane_of < rows, pick, 0.0)
        norm = norm + jnp.dot(
            mine, pick, preferred_element_type=f32, precision=lax.Precision.HIGHEST
        )
    norm_ref[...] = norm[0:TOK, :]


def call(body, out_shape, in_specs, scratch=(), room=SMALL):
    many = isinstance(out_shape, tuple)
    return pl.pallas_call(
        body,
        out_shape=out_shape,
        in_specs=in_specs,
        out_specs=(VMEM,) * len(out_shape) if many else VMEM,
        scratch_shapes=list(scratch),
        compiler_params=pltpu.CompilerParams(vmem_limit_bytes=room * 2**20),
    )


def on_device(queries, keys, values, lengths):
    shape = jax.ShapeDtypeStruct
    same_core = [[2 * i + c for i in range(CHIPS)] for c in range(CORES)]
    swap = [(i, i ^ 1) for i in range(CHIPS * CORES)]
    parts = lax.axis_size("head")

    sent = call(spread_body, shape((CHIPS, KV * ROWS, DH), bf16), [VMEM])(queries)
    q_own = lax.all_to_all(sent, "ctx", 0, 0, tiled=True, axis_index_groups=same_core)
    q_other = lax.ppermute(q_own, "ctx", swap)
    acc = shape((KV, AUG, HALF), f32)
    own, other = call(
        attend_body,
        (acc, acc),
        [SMEM, VMEM, VMEM, ANY, ANY],
        [
            pltpu.VMEM((CTX, KV * DH), bf16),
            pltpu.VMEM((CTX, KV * DH), bf16),
            pltpu.VMEM((KV, 2 * DH, COLS), bf16),
            pltpu.VMEM((AUG, max(CHUNKS)), bf16),
            pltpu.SemaphoreType.DMA((len(CHUNKS),)),
            pltpu.SemaphoreType.DMA((len(CHUNKS),)),
        ],
        LARGE,
    )(lengths, q_own, q_other, keys, values)
    partner = lax.ppermute(other, "ctx", swap)
    sent = call(pair_body, shape((CHIPS, MSG, DH), jnp.int16), [VMEM, VMEM])(own, partner)
    got = lax.all_to_all(sent, "ctx", 0, 0, tiled=True, axis_index_groups=same_core)
    sent = call(merge_body, shape((parts, MSG, DH), bf16), [VMEM])(got)
    got = lax.all_to_all(sent, "head", 0, 0, tiled=True)
    heads = parts * KV * GRP
    return call(finish_body, (shape((TOK, heads * DH), bf16), shape((TOK, heads), f32)), [VMEM])(
        got
    )


def solution(mesh):
    return jax.shard_map(
        on_device,
        mesh=mesh,
        in_specs=(P("ctx", "head"), P("ctx", "head"), P("ctx", "head"), P("ctx")),
        out_specs=(P("ctx", None), P("ctx", None)),
        check_vma=False,
    )
```

```python
import functools
import math

import jax
import jax.numpy as jnp
from jax import lax
from jax.experimental import pallas as pl
from jax.experimental.pallas import tpu as pltpu
from jax.sharding import PartitionSpec as P

DH = 128
f32, bf16 = jnp.float32, jnp.bfloat16
LOG2E = 1.4426950408889634
LN2 = 0.6931471805599453
TO_LOG2 = LOG2E / math.sqrt(DH)

CHIPS, CORES = 16, 2
TOK, GRP, KV = 6, 8, 2
ROWS = TOK * GRP
HALF = CHIPS * ROWS
COLS = CORES * HALF
CTX = 8192
FIRST, LATER = (1024, 3072, 4096), (4096, 4096)
LROW, MROW, AUG = DH, DH + 8, DH + 16
RIM = 16
MSG = KV * ROWS + RIM
STEPS = 32766.0

VMEM = pl.BlockSpec(memory_space=pltpu.VMEM)
SMEM = pl.BlockSpec(memory_space=pltpu.SMEM)
ANY = pl.BlockSpec(memory_space=pl.ANY)
SMALL, LARGE = 8, 40


def spread_body(q_ref, out_ref):
    q = q_ref[...].astype(f32)
    rows = jnp.concatenate([q[:, i * DH : (i + 1) * DH] for i in range(KV * GRP)], axis=0)
    out_ref[...] = jnp.broadcast_to(rows.astype(bf16)[None], out_ref.shape)


def attend_body(fresh, *refs):
    if fresh:
        len_ref, q_ref, k_hbm, v_hbm, out_ref, k_ref, vt_ref, qt, v_ref, ksem, vsem = refs
        steps = FIRST
    else:
        len_ref, q_ref, k_ref, vt_ref, out_ref, qt = refs
        steps = LATER
    valid = len_ref[0]
    starts = [sum(steps[:c]) for c in range(len(steps))]

    def copies(c):
        part = pl.ds(starts[c], steps[c])
        return (
            pltpu.make_async_copy(v_hbm.at[part], v_ref.at[part], vsem.at[c]),
            pltpu.make_async_copy(k_hbm.at[part], k_ref.at[part], ksem.at[c]),
        )

    if fresh:
        for c in range(len(steps)):
            for copy in copies(c):
                copy.start()

    def turn_values(h, c):
        part = slice(starts[c], starts[c] + steps[c])
        ok = lax.broadcasted_iota(jnp.int32, (1, steps[c]), 1) + starts[c] < valid
        v = v_ref[part, h * DH : (h + 1) * DH].T.astype(f32)
        vt_ref[h, 0:DH, part] = jnp.where(ok, v, 0.0).astype(bf16)
        ones = jnp.broadcast_to(jnp.where(ok, 1.0, 0.0), (AUG - DH, steps[c]))
        vt_ref[h, DH:AUG, part] = ones.astype(bf16)

    for h in range(KV):
        x = q_ref[:, h * ROWS : (h + 1) * ROWS, :].reshape(HALF, DH).astype(f32).T * TO_LOG2
        high = x.astype(bf16)
        qt[h, 0:DH, :] = high
        qt[h, DH : 2 * DH, :] = (x - high.astype(f32)).astype(bf16)

    def scores(h, first, size):
        k = k_ref[pl.ds(first, size), h * DH : (h + 1) * DH]
        return jnp.dot(jnp.concatenate([k, k], axis=1), qt[h], preferred_element_type=f32)

    for c in range(len(steps)):
        if fresh and c < 2:
            for later in range(c, len(steps) if c else 1):
                for copy in copies(later):
                    copy.wait()
        for h in range(KV):
            if fresh:
                turn_values(h, c)
            p = jnp.exp2(scores(h, starts[c], steps[c])).astype(bf16)
            v = vt_ref[h, :, pl.ds(starts[c], steps[c])]
            pv = jnp.dot(v, p, preferred_element_type=f32)
            if c == 0:
                out_ref[h] = pv
            else:
                out_ref[h] += pv

    wrong = jnp.zeros((1, HALF), f32)
    for h in range(KV):
        total = out_ref[h, LROW : LROW + 1, :]
        fine = (total > 2.0**-60) & (total < 2.0**90)
        wrong = wrong + jnp.where(fine, 0.0, 1.0)
        out_ref[h, MROW:AUG, :] = jnp.zeros((AUG - MROW, HALF), f32)

    @pl.when(jnp.sum(wrong) > 0.5)
    def _():
        size = 512

        def masked(h, first):
            pos = lax.broadcasted_iota(jnp.int32, (size, 1), 0) + first
            return jnp.where(pos < valid, scores(h, first, size), -1e30)

        for h in range(KV):

            def top(c, best):
                s = masked(h, pl.multiple_of(c * size, size))
                return jnp.maximum(best, jnp.max(s, axis=0, keepdims=True))

            peak = lax.fori_loop(0, CTX // size, top, jnp.full((1, HALF), -1e30, f32))
            out_ref[h] = jnp.zeros((AUG, HALF), f32)

            def add(c, carry):
                first = pl.multiple_of(c * size, size)
                p = jnp.exp2(masked(h, first) - peak).astype(bf16)
                v = vt_ref[h, :, pl.ds(first, size)]
                out_ref[h] += jnp.dot(v, p, preferred_element_type=f32)
                return carry

            lax.fori_loop(0, CTX // size, add, 0)
            out_ref[h, MROW:AUG, :] = jnp.broadcast_to(peak, (AUG - MROW, HALF))


def pair_body(a_all, b_all, out_ref):
    for h in range(KV):
        a_ref, b_ref = a_all.at[h], b_all.at[h]
        ma, mb = a_ref[MROW : MROW + 1, :], b_ref[MROW : MROW + 1, :]
        top = jnp.maximum(ma, mb)
        wa, wb = jnp.exp2(ma - top), jnp.exp2(mb - top)
        total = wa * a_ref[LROW : LROW + 1, :] + wb * b_ref[LROW : LROW + 1, :]
        num = a_ref[0:DH, :] * (wa / total) + b_ref[0:DH, :] * (wb / total)
        size = jnp.max(jnp.abs(num), axis=0, keepdims=True)
        power = jnp.ceil(jnp.log2(jnp.maximum(size * 1.0001, 2.0**-100)))
        num = num * (jnp.exp2(-power) * STEPS)
        norm = (top + jnp.log2(total)) * 16.0
        coarse = jnp.floor(norm)
        fine = jnp.floor((norm - coarse) * 32767.0)
        rim = jnp.concatenate([coarse, fine, power, jnp.zeros((RIM - 3, HALF), f32)], axis=0)
        rim = rim.astype(jnp.int32)
        codes = jnp.round(num.T).astype(jnp.int32).astype(jnp.int16)
        out_ref[:, h * ROWS : (h + 1) * ROWS, :] = codes.reshape(CHIPS, ROWS, DH)
        for c in range(CHIPS):
            out_ref[c, KV * ROWS : MSG, h * ROWS : (h + 1) * ROWS] = rim[
                :, c * ROWS : (c + 1) * ROWS
            ].astype(jnp.int16)


def merge_body(in_ref, out_ref):
    rows = KV * ROWS
    rim = in_ref[:, rows:MSG, :].astype(jnp.int32).astype(f32)
    used = lax.broadcasted_iota(jnp.int32, (CHIPS, DH), 1) < rows
    norm = jnp.where(used, rim[:, 0, :] * 0.0625 + rim[:, 1, :] * (0.0625 / 32767.0), 0.0)
    power = jnp.where(used, rim[:, 2, :], 0.0)
    top = jnp.max(norm, axis=0, keepdims=True)
    w = jnp.exp2(norm - top)
    total = jnp.sum(w, axis=0, keepdims=True)
    w = (w * jnp.exp2(power) / (total * STEPS)).T
    o = jnp.zeros((rows, DH), f32)
    for c in range(CHIPS):
        o = o + in_ref[c, 0:rows, :].astype(jnp.int32).astype(f32) * w[0:rows, c : c + 1]
    parts = out_ref.shape[0]
    out_ref[:, 0:rows, :] = jnp.broadcast_to(o.astype(bf16)[None], (parts, rows, DH))
    norm = (top + jnp.log2(total)) * LN2
    pieces = []
    for _ in range(3):
        piece = norm.astype(bf16).astype(f32)
        pieces.append(piece)
        norm = norm - piece
    rim = jnp.concatenate([*pieces, jnp.zeros((RIM - 3, DH), f32)], axis=0).astype(bf16)
    out_ref[:, rows:MSG, :] = jnp.broadcast_to(rim[None], (parts, RIM, DH))


def finish_body(in_ref, mixed_ref, norm_ref):
    rows, heads = KV * ROWS, KV * GRP
    parts = in_ref.shape[0]
    token = lax.broadcasted_iota(jnp.int32, (8, DH), 0)
    lane = lax.broadcasted_iota(jnp.int32, (8, DH), 1)
    lane_of = lax.broadcasted_iota(jnp.int32, (DH, parts * heads), 0)
    head_of = lax.broadcasted_iota(jnp.int32, (DH, parts * heads), 1)
    norm = jnp.zeros((8, parts * heads), f32)
    for z in range(parts):
        o = in_ref[z, 0:rows, :].astype(f32)
        for i in range(heads):
            mixed_ref[:, (z * heads + i) * DH : (z * heads + i + 1) * DH] = o[
                i * TOK : (i + 1) * TOK, :
            ].astype(bf16)
        rim = in_ref[z, rows:MSG, :].astype(f32)
        mine = jnp.where((lane % TOK == token) & (lane < rows), rim[0:1] + rim[1:2] + rim[2:3], 0.0)
        pick = jnp.where(lane_of // TOK + z * heads == head_of, 1.0, 0.0)
        pick = jnp.where(lane_of < rows, pick, 0.0)
        norm = norm + jnp.dot(
            mine, pick, preferred_element_type=f32, precision=lax.Precision.HIGHEST
        )
    norm_ref[...] = norm[0:TOK, :]


def call(body, out_shape, in_specs, scratch=(), room=SMALL, cost=None):
    many = isinstance(out_shape, tuple)
    return pl.pallas_call(
        body,
        out_shape=out_shape,
        in_specs=in_specs,
        out_specs=(VMEM,) * len(out_shape) if many else VMEM,
        scratch_shapes=list(scratch),
        cost_estimate=cost,
        compiler_params=pltpu.CompilerParams(vmem_limit_bytes=room * 2**20),
    )


def hbm(x):
    return pltpu.with_memory_space_constraint(x, pltpu.HBM)


def on_device(queries, keys, values, lengths):
    shape = jax.ShapeDtypeStruct
    same_core = [[2 * i + c for i in range(CHIPS)] for c in range(CORES)]
    swap = [(i, i ^ 1) for i in range(CHIPS * CORES)]
    parts = lax.axis_size("head")

    sent = call(spread_body, shape((CHIPS, KV * ROWS, DH), bf16), [VMEM])(queries)
    q_own = lax.all_to_all(sent, "ctx", 0, 0, tiled=True, axis_index_groups=same_core)
    q_other = lax.ppermute(q_own, "ctx", swap)

    def attend(fresh, *args):
        acc = shape((KV, AUG, HALF), f32)
        handed = (shape((CTX, KV * DH), bf16), shape((KV, AUG, CTX), bf16))
        scratch = [pltpu.VMEM((KV, 2 * DH, HALF), bf16)]
        if fresh:
            scratch += [pltpu.VMEM((CTX, KV * DH), bf16)]
            scratch += [pltpu.SemaphoreType.DMA((len(FIRST),))] * 2
        return call(
            functools.partial(attend_body, fresh),
            (acc, *handed) if fresh else acc,
            [SMEM, VMEM, ANY, ANY] if fresh else [SMEM, VMEM, VMEM, VMEM],
            scratch,
            LARGE,
            pl.CostEstimate(
                flops=KV * 6 * DH * HALF * CTX, bytes_accessed=2**20, transcendentals=KV * HALF * CTX
            ),
        )(*args)

    other, k, vt = attend(True, lengths, q_other, hbm(keys), hbm(values))
    partner = lax.ppermute(other, "ctx", swap)
    own = attend(False, lengths, q_own, k, vt)
    sent = call(pair_body, shape((CHIPS, MSG, DH), jnp.int16), [VMEM] * 2)(own, partner)
    got = lax.all_to_all(sent, "ctx", 0, 0, tiled=True, axis_index_groups=same_core)
    sent = call(merge_body, shape((parts, MSG, DH), bf16), [VMEM])(got)
    got = lax.all_to_all(sent, "head", 0, 0, tiled=True)
    heads = parts * KV * GRP
    return call(finish_body, (shape((TOK, heads * DH), bf16), shape((TOK, heads), f32)), [VMEM])(
        got
    )


def solution(mesh):
    return jax.shard_map(
        on_device,
        mesh=mesh,
        in_specs=(P("ctx", "head"), P("ctx", "head"), P("ctx", "head"), P("ctx")),
        out_specs=(P("ctx", None), P("ctx", None)),
        check_vma=False,
    )
```

```python
import math

import jax
import jax.numpy as jnp
from jax import lax
from jax.experimental import pallas as pl
from jax.experimental.pallas import tpu as pltpu
from jax.sharding import PartitionSpec as P

DH = 128
f32, bf16 = jnp.float32, jnp.bfloat16
LOG2E = 1.4426950408889634
LN2 = 0.6931471805599453
TO_LOG2 = LOG2E / math.sqrt(DH)

CHIPS, CORES = 16, 2
TOK, GRP, KV = 6, 8, 2
ROWS = TOK * GRP
HALF = CHIPS * ROWS
COLS = CORES * HALF
CTX = 8192
SPANS = (4096, 4096)
TURN = 2048
LROW, MROW, AUG = DH, DH + 8, DH + 16
RIM = 16
MSG = KV * ROWS + RIM
STEPS = 32766.0

VMEM = pl.BlockSpec(memory_space=pltpu.VMEM)
ANY = pl.BlockSpec(memory_space=pl.ANY)
SMALL, MIDDLE, LARGE = 8, 16, 40


def spread_body(q_ref, out_ref):
    q = q_ref[...].astype(f32)
    rows = jnp.concatenate([q[:, i * DH : (i + 1) * DH] for i in range(KV * GRP)], axis=0)
    out_ref[...] = jnp.broadcast_to(rows.astype(bf16)[None], out_ref.shape)


def prepare_body(len_ref, v_ref, _, vt_ref):
    valid = len_ref[0:1, 0:1]
    for c in range(CTX // TURN):
        part = slice(c * TURN, (c + 1) * TURN)
        ok = lax.broadcasted_iota(jnp.int32, (1, TURN), 1) + c * TURN < valid
        ones = jnp.broadcast_to(jnp.where(ok, 1.0, 0.0), (AUG - DH, TURN))
        for h in range(KV):
            v = v_ref[part, h * DH : (h + 1) * DH].T.astype(f32)
            vt_ref[h, 0:DH, part] = jnp.where(ok, v, 0.0).astype(bf16)
            vt_ref[h, DH:AUG, part] = ones.astype(bf16)


def attend_body(len_ref, q_ref, k_ref, vt_ref, out_ref, qt):
    valid = len_ref[0:1, 0:1]
    starts = [sum(SPANS[:c]) for c in range(len(SPANS))]

    for h in range(KV):
        x = q_ref[:, h * ROWS : (h + 1) * ROWS, :].reshape(HALF, DH).astype(f32).T * TO_LOG2
        high = x.astype(bf16)
        qt[h, 0:DH, :] = high
        qt[h, DH : 2 * DH, :] = (x - high.astype(f32)).astype(bf16)

    def scores(h, first, size):
        k = k_ref[pl.ds(first, size), h * DH : (h + 1) * DH]
        return jnp.dot(jnp.concatenate([k, k], axis=1), qt[h], preferred_element_type=f32)

    for c in range(len(SPANS)):
        for h in range(KV):
            p = jnp.exp2(scores(h, starts[c], SPANS[c])).astype(bf16)
            v = vt_ref[h, :, pl.ds(starts[c], SPANS[c])]
            pv = jnp.dot(v, p, preferred_element_type=f32)
            if c == 0:
                out_ref[h] = pv
            else:
                out_ref[h] += pv

    wrong = jnp.zeros((1, HALF), f32)
    for h in range(KV):
        total = out_ref[h, LROW : LROW + 1, :]
        fine = (total > 2.0**-60) & (total < 2.0**90)
        wrong = wrong + jnp.where(fine, 0.0, 1.0)
        out_ref[h, MROW:AUG, :] = jnp.zeros((AUG - MROW, HALF), f32)

    @pl.when(jnp.sum(wrong) > 0.5)
    def _():
        size = 512

        def masked(h, first):
            pos = lax.broadcasted_iota(jnp.int32, (size, 1), 0) + first
            return jnp.where(pos < valid, scores(h, first, size), -1e30)

        for h in range(KV):

            def top(c, best):
                s = masked(h, pl.multiple_of(c * size, size))
                return jnp.maximum(best, jnp.max(s, axis=0, keepdims=True))

            peak = lax.fori_loop(0, CTX // size, top, jnp.full((1, HALF), -1e30, f32))
            out_ref[h] = jnp.zeros((AUG, HALF), f32)

            def add(c, carry):
                first = pl.multiple_of(c * size, size)
                p = jnp.exp2(masked(h, first) - peak).astype(bf16)
                v = vt_ref[h, :, pl.ds(first, size)]
                out_ref[h] += jnp.dot(v, p, preferred_element_type=f32)
                return carry

            lax.fori_loop(0, CTX // size, add, 0)
            out_ref[h, MROW:AUG, :] = jnp.broadcast_to(peak, (AUG - MROW, HALF))


def pair_body(a_all, b_all, out_ref):
    for h in range(KV):
        a_ref, b_ref = a_all.at[h], b_all.at[h]
        ma, mb = a_ref[MROW : MROW + 1, :], b_ref[MROW : MROW + 1, :]
        top = jnp.maximum(ma, mb)
        wa, wb = jnp.exp2(ma - top), jnp.exp2(mb - top)
        total = wa * a_ref[LROW : LROW + 1, :] + wb * b_ref[LROW : LROW + 1, :]
        num = a_ref[0:DH, :] * (wa / total) + b_ref[0:DH, :] * (wb / total)
        size = jnp.max(jnp.abs(num), axis=0, keepdims=True)
        power = jnp.ceil(jnp.log2(jnp.maximum(size * 1.0001, 2.0**-100)))
        num = num * (jnp.exp2(-power) * STEPS)
        norm = (top + jnp.log2(total)) * 16.0
        coarse = jnp.floor(norm)
        fine = jnp.floor((norm - coarse) * 32767.0)
        rim = jnp.concatenate([coarse, fine, power, jnp.zeros((RIM - 3, HALF), f32)], axis=0)
        rim = rim.astype(jnp.int32)
        codes = jnp.round(num.T).astype(jnp.int32).astype(jnp.int16)
        out_ref[:, h * ROWS : (h + 1) * ROWS, :] = codes.reshape(CHIPS, ROWS, DH)
        for c in range(CHIPS):
            out_ref[c, KV * ROWS : MSG, h * ROWS : (h + 1) * ROWS] = rim[
                :, c * ROWS : (c + 1) * ROWS
            ].astype(jnp.int16)


def merge_body(in_ref, out_ref):
    rows = KV * ROWS
    rim = in_ref[:, rows:MSG, :].astype(jnp.int32).astype(f32)
    used = lax.broadcasted_iota(jnp.int32, (CHIPS, DH), 1) < rows
    norm = jnp.where(used, rim[:, 0, :] * 0.0625 + rim[:, 1, :] * (0.0625 / 32767.0), 0.0)
    power = jnp.where(used, rim[:, 2, :], 0.0)
    top = jnp.max(norm, axis=0, keepdims=True)
    w = jnp.exp2(norm - top)
    total = jnp.sum(w, axis=0, keepdims=True)
    w = (w * jnp.exp2(power) / (total * STEPS)).T
    o = jnp.zeros((rows, DH), f32)
    for c in range(CHIPS):
        o = o + in_ref[c, 0:rows, :].astype(jnp.int32).astype(f32) * w[0:rows, c : c + 1]
    parts = out_ref.shape[0]
    out_ref[:, 0:rows, :] = jnp.broadcast_to(o.astype(bf16)[None], (parts, rows, DH))
    norm = (top + jnp.log2(total)) * LN2
    pieces = []
    for _ in range(3):
        piece = norm.astype(bf16).astype(f32)
        pieces.append(piece)
        norm = norm - piece
    rim = jnp.concatenate([*pieces, jnp.zeros((RIM - 3, DH), f32)], axis=0).astype(bf16)
    out_ref[:, rows:MSG, :] = jnp.broadcast_to(rim[None], (parts, RIM, DH))


def finish_body(in_ref, mixed_ref, norm_ref):
    rows, heads = KV * ROWS, KV * GRP
    parts = in_ref.shape[0]
    token = lax.broadcasted_iota(jnp.int32, (8, DH), 0)
    lane = lax.broadcasted_iota(jnp.int32, (8, DH), 1)
    lane_of = lax.broadcasted_iota(jnp.int32, (DH, parts * heads), 0)
    head_of = lax.broadcasted_iota(jnp.int32, (DH, parts * heads), 1)
    norm = jnp.zeros((8, parts * heads), f32)
    for z in range(parts):
        o = in_ref[z, 0:rows, :].astype(f32)
        for i in range(heads):
            mixed_ref[:, (z * heads + i) * DH : (z * heads + i + 1) * DH] = o[
                i * TOK : (i + 1) * TOK, :
            ].astype(bf16)
        rim = in_ref[z, rows:MSG, :].astype(f32)
        mine = jnp.where((lane % TOK == token) & (lane < rows), rim[0:1] + rim[1:2] + rim[2:3], 0.0)
        pick = jnp.where(lane_of // TOK + z * heads == head_of, 1.0, 0.0)
        pick = jnp.where(lane_of < rows, pick, 0.0)
        norm = norm + jnp.dot(
            mine, pick, preferred_element_type=f32, precision=lax.Precision.HIGHEST
        )
    norm_ref[...] = norm[0:TOK, :]


def call(body, out_shape, in_specs, scratch=(), room=SMALL, cost=None):
    many = isinstance(out_shape, tuple)
    return pl.pallas_call(
        body,
        out_shape=out_shape,
        in_specs=in_specs,
        out_specs=(VMEM,) * len(out_shape) if many else VMEM,
        scratch_shapes=list(scratch),
        cost_estimate=cost,
        compiler_params=pltpu.CompilerParams(vmem_limit_bytes=room * 2**20),
    )


def vmem(x):
    return pltpu.with_memory_space_constraint(x, pltpu.VMEM)


def on_device(queries, keys, values, lengths):
    shape = jax.ShapeDtypeStruct
    same_core = [[2 * i + c for i in range(CHIPS)] for c in range(CORES)]
    swap = [(i, i ^ 1) for i in range(CHIPS * CORES)]
    parts = lax.axis_size("head")

    lengths = lax.ppermute(jnp.broadcast_to(lengths, (8, DH)), "ctx", swap)
    keys, values, lengths = lax.optimization_barrier((keys, values, lengths))
    keys, values = (vmem(lax.ppermute(x, "ctx", swap)) for x in (keys, values))
    sent = call(spread_body, shape((CHIPS, KV * ROWS, DH), bf16), [VMEM])(queries)
    q_own = lax.all_to_all(sent, "ctx", 0, 0, tiled=True, axis_index_groups=same_core)
    q_other = lax.ppermute(q_own, "ctx", swap)

    turned = call(
        prepare_body,
        shape((KV, AUG, CTX), bf16),
        [VMEM, VMEM, ANY],
        (),
        MIDDLE,
        pl.CostEstimate(flops=0, bytes_accessed=9 * 2**20, transcendentals=0),
    )(lengths, values, q_own)

    def attend(q):
        return call(
            attend_body,
            shape((KV, AUG, HALF), f32),
            [VMEM, VMEM, VMEM, VMEM],
            [pltpu.VMEM((KV, 2 * DH, HALF), bf16)],
            LARGE,
            pl.CostEstimate(
                flops=KV * 6 * DH * HALF * CTX, bytes_accessed=2**20, transcendentals=KV * HALF * CTX
            ),
        )(lengths, q, keys, turned)

    other = attend(q_other)
    partner = lax.ppermute(other, "ctx", swap)
    own = attend(q_own)
    sent = call(pair_body, shape((CHIPS, MSG, DH), jnp.int16), [VMEM] * 2)(own, partner)
    got = lax.all_to_all(sent, "ctx", 0, 0, tiled=True, axis_index_groups=same_core)
    sent = call(merge_body, shape((parts, MSG, DH), bf16), [VMEM])(got)
    got = lax.all_to_all(sent, "head", 0, 0, tiled=True)
    heads = parts * KV * GRP
    return call(finish_body, (shape((TOK, heads * DH), bf16), shape((TOK, heads), f32)), [VMEM])(
        got
    )


def solution(mesh):
    return jax.shard_map(
        on_device,
        mesh=mesh,
        in_specs=(P("ctx", "head"), P("ctx", "head"), P("ctx", "head"), P("ctx")),
        out_specs=(P("ctx", None), P("ctx", None)),
        check_vma=False,
    )
```

```python
import math

import jax
import jax.numpy as jnp
from jax import lax
from jax.experimental import pallas as pl
from jax.experimental.pallas import tpu as pltpu
from jax.sharding import PartitionSpec as P

DH = 128
f32, bf16 = jnp.float32, jnp.bfloat16
LOG2E = 1.4426950408889634
LN2 = 0.6931471805599453
TO_LOG2 = LOG2E / math.sqrt(DH)

CHIPS, CORES = 16, 2
TOK, GRP, KV = 6, 8, 2
ROWS = TOK * GRP
HALF = CHIPS * ROWS
COLS = CORES * HALF
CTX = 8192
SPANS = (4096, 4096)
TURNS = (1024, 1024, 2048, 2048, 2048)
LROW, MROW, AUG = DH, DH + 8, DH + 16
RIM = 16
MSG = KV * ROWS + RIM
STEPS = 32766.0

VMEM = pl.BlockSpec(memory_space=pltpu.VMEM)
SMEM = pl.BlockSpec(memory_space=pltpu.SMEM)
ANY = pl.BlockSpec(memory_space=pl.ANY)
SMALL, MIDDLE, LARGE = 8, 16, 40


def spread_body(q_ref, out_ref):
    q = q_ref[...].astype(f32)
    rows = jnp.concatenate([q[:, i * DH : (i + 1) * DH] for i in range(KV * GRP)], axis=0)
    out_ref[...] = jnp.broadcast_to(rows.astype(bf16)[None], out_ref.shape)


def prepare_body(len_ref, k_hbm, v_hbm, _, k_ref, vt_ref, v_ref, ksem, vsem):
    starts = [sum(TURNS[:c]) for c in range(len(TURNS))]

    def values(c):
        part = pl.ds(starts[c], TURNS[c])
        return pltpu.make_async_copy(v_hbm.at[part], v_ref.at[part], vsem.at[c])

    keys = pltpu.make_async_copy(k_hbm, k_ref, ksem)
    for c in range(len(TURNS)):
        values(c).start()
    keys.start()
    valid = len_ref[0]
    for c in range(len(TURNS)):
        values(c).wait()
        part = slice(starts[c], starts[c] + TURNS[c])
        ok = lax.broadcasted_iota(jnp.int32, (1, TURNS[c]), 1) + starts[c] < valid
        ones = jnp.broadcast_to(jnp.where(ok, 1.0, 0.0), (AUG - DH, TURNS[c]))
        for h in range(KV):
            v = v_ref[part, h * DH : (h + 1) * DH].T.astype(f32)
            vt_ref[h, 0:DH, part] = jnp.where(ok, v, 0.0).astype(bf16)
            vt_ref[h, DH:AUG, part] = ones.astype(bf16)
    keys.wait()


def attend_body(len_ref, q_ref, k_ref, vt_ref, out_ref, qt):
    valid = len_ref[0]
    starts = [sum(SPANS[:c]) for c in range(len(SPANS))]

    for h in range(KV):
        x = q_ref[:, h * ROWS : (h + 1) * ROWS, :].reshape(HALF, DH).astype(f32).T * TO_LOG2
        high = x.astype(bf16)
        qt[h, 0:DH, :] = high
        qt[h, DH : 2 * DH, :] = (x - high.astype(f32)).astype(bf16)

    def scores(h, first, size):
        k = k_ref[pl.ds(first, size), h * DH : (h + 1) * DH]
        return jnp.dot(jnp.concatenate([k, k], axis=1), qt[h], preferred_element_type=f32)

    for c in range(len(SPANS)):
        for h in range(KV):
            p = jnp.exp2(scores(h, starts[c], SPANS[c])).astype(bf16)
            v = vt_ref[h, :, pl.ds(starts[c], SPANS[c])]
            pv = jnp.dot(v, p, preferred_element_type=f32)
            if c == 0:
                out_ref[h] = pv
            else:
                out_ref[h] += pv

    wrong = jnp.zeros((1, HALF), f32)
    for h in range(KV):
        total = out_ref[h, LROW : LROW + 1, :]
        fine = (total > 2.0**-60) & (total < 2.0**90)
        wrong = wrong + jnp.where(fine, 0.0, 1.0)
        out_ref[h, MROW:AUG, :] = jnp.zeros((AUG - MROW, HALF), f32)

    @pl.when(jnp.sum(wrong) > 0.5)
    def _():
        size = 512

        def masked(h, first):
            pos = lax.broadcasted_iota(jnp.int32, (size, 1), 0) + first
            return jnp.where(pos < valid, scores(h, first, size), -1e30)

        for h in range(KV):

            def top(c, best):
                s = masked(h, pl.multiple_of(c * size, size))
                return jnp.maximum(best, jnp.max(s, axis=0, keepdims=True))

            peak = lax.fori_loop(0, CTX // size, top, jnp.full((1, HALF), -1e30, f32))
            out_ref[h] = jnp.zeros((AUG, HALF), f32)

            def add(c, carry):
                first = pl.multiple_of(c * size, size)
                p = jnp.exp2(masked(h, first) - peak).astype(bf16)
                v = vt_ref[h, :, pl.ds(first, size)]
                out_ref[h] += jnp.dot(v, p, preferred_element_type=f32)
                return carry

            lax.fori_loop(0, CTX // size, add, 0)
            out_ref[h, MROW:AUG, :] = jnp.broadcast_to(peak, (AUG - MROW, HALF))


def pair_body(a_all, b_all, out_ref):
    for h in range(KV):
        a_ref, b_ref = a_all.at[h], b_all.at[h]
        ma, mb = a_ref[MROW : MROW + 1, :], b_ref[MROW : MROW + 1, :]
        top = jnp.maximum(ma, mb)
        wa, wb = jnp.exp2(ma - top), jnp.exp2(mb - top)
        total = wa * a_ref[LROW : LROW + 1, :] + wb * b_ref[LROW : LROW + 1, :]
        num = a_ref[0:DH, :] * (wa / total) + b_ref[0:DH, :] * (wb / total)
        size = jnp.max(jnp.abs(num), axis=0, keepdims=True)
        power = jnp.ceil(jnp.log2(jnp.maximum(size * 1.0001, 2.0**-100)))
        num = num * (jnp.exp2(-power) * STEPS)
        norm = (top + jnp.log2(total)) * 16.0
        coarse = jnp.floor(norm)
        fine = jnp.floor((norm - coarse) * 32767.0)
        rim = jnp.concatenate([coarse, fine, power, jnp.zeros((RIM - 3, HALF), f32)], axis=0)
        rim = rim.astype(jnp.int32)
        codes = jnp.round(num.T).astype(jnp.int32).astype(jnp.int16)
        out_ref[:, h * ROWS : (h + 1) * ROWS, :] = codes.reshape(CHIPS, ROWS, DH)
        for c in range(CHIPS):
            out_ref[c, KV * ROWS : MSG, h * ROWS : (h + 1) * ROWS] = rim[
                :, c * ROWS : (c + 1) * ROWS
            ].astype(jnp.int16)


def merge_body(in_ref, out_ref):
    rows = KV * ROWS
    rim = in_ref[:, rows:MSG, :].astype(jnp.int32).astype(f32)
    used = lax.broadcasted_iota(jnp.int32, (CHIPS, DH), 1) < rows
    norm = jnp.where(used, rim[:, 0, :] * 0.0625 + rim[:, 1, :] * (0.0625 / 32767.0), 0.0)
    power = jnp.where(used, rim[:, 2, :], 0.0)
    top = jnp.max(norm, axis=0, keepdims=True)
    w = jnp.exp2(norm - top)
    total = jnp.sum(w, axis=0, keepdims=True)
    w = (w * jnp.exp2(power) / (total * STEPS)).T
    o = jnp.zeros((rows, DH), f32)
    for c in range(CHIPS):
        o = o + in_ref[c, 0:rows, :].astype(jnp.int32).astype(f32) * w[0:rows, c : c + 1]
    parts = out_ref.shape[0]
    out_ref[:, 0:rows, :] = jnp.broadcast_to(o.astype(bf16)[None], (parts, rows, DH))
    norm = (top + jnp.log2(total)) * LN2
    pieces = []
    for _ in range(3):
        piece = norm.astype(bf16).astype(f32)
        pieces.append(piece)
        norm = norm - piece
    rim = jnp.concatenate([*pieces, jnp.zeros((RIM - 3, DH), f32)], axis=0).astype(bf16)
    out_ref[:, rows:MSG, :] = jnp.broadcast_to(rim[None], (parts, RIM, DH))


def finish_body(in_ref, mixed_ref, norm_ref):
    rows, heads = KV * ROWS, KV * GRP
    parts = in_ref.shape[0]
    token = lax.broadcasted_iota(jnp.int32, (8, DH), 0)
    lane = lax.broadcasted_iota(jnp.int32, (8, DH), 1)
    lane_of = lax.broadcasted_iota(jnp.int32, (DH, parts * heads), 0)
    head_of = lax.broadcasted_iota(jnp.int32, (DH, parts * heads), 1)
    norm = jnp.zeros((8, parts * heads), f32)
    for z in range(parts):
        o = in_ref[z, 0:rows, :].astype(f32)
        for i in range(heads):
            mixed_ref[:, (z * heads + i) * DH : (z * heads + i + 1) * DH] = o[
                i * TOK : (i + 1) * TOK, :
            ].astype(bf16)
        rim = in_ref[z, rows:MSG, :].astype(f32)
        mine = jnp.where((lane % TOK == token) & (lane < rows), rim[0:1] + rim[1:2] + rim[2:3], 0.0)
        pick = jnp.where(lane_of // TOK + z * heads == head_of, 1.0, 0.0)
        pick = jnp.where(lane_of < rows, pick, 0.0)
        norm = norm + jnp.dot(
            mine, pick, preferred_element_type=f32, precision=lax.Precision.HIGHEST
        )
    norm_ref[...] = norm[0:TOK, :]


def call(body, out_shape, in_specs, scratch=(), room=SMALL, cost=None):
    many = isinstance(out_shape, tuple)
    return pl.pallas_call(
        body,
        out_shape=out_shape,
        in_specs=in_specs,
        out_specs=(VMEM,) * len(out_shape) if many else VMEM,
        scratch_shapes=list(scratch),
        cost_estimate=cost,
        compiler_params=pltpu.CompilerParams(vmem_limit_bytes=room * 2**20),
    )


def hbm(x):
    return pltpu.with_memory_space_constraint(x, pltpu.HBM)


def on_device(queries, keys, values, lengths):
    shape = jax.ShapeDtypeStruct
    same_core = [[2 * i + c for i in range(CHIPS)] for c in range(CORES)]
    swap = [(i, i ^ 1) for i in range(CHIPS * CORES)]
    parts = lax.axis_size("head")

    sent = call(spread_body, shape((CHIPS, KV * ROWS, DH), bf16), [VMEM])(hbm(queries))
    q_own = lax.all_to_all(sent, "ctx", 0, 0, tiled=True, axis_index_groups=same_core)
    q_other = lax.ppermute(q_own, "ctx", swap)

    keys, turned = call(
        prepare_body,
        (shape((CTX, KV * DH), bf16), shape((KV, AUG, CTX), bf16)),
        [SMEM, ANY, ANY, ANY],
        [
            pltpu.VMEM((CTX, KV * DH), bf16),
            pltpu.SemaphoreType.DMA,
            pltpu.SemaphoreType.DMA((len(TURNS),)),
        ],
        MIDDLE,
        pl.CostEstimate(flops=0, bytes_accessed=17 * 2**20, transcendentals=0),
    )(lengths, hbm(keys), hbm(values), q_own)

    def attend(q):
        return call(
            attend_body,
            shape((KV, AUG, HALF), f32),
            [SMEM, VMEM, VMEM, VMEM],
            [pltpu.VMEM((KV, 2 * DH, HALF), bf16)],
            LARGE,
            pl.CostEstimate(
                flops=KV * 6 * DH * HALF * CTX, bytes_accessed=2**20, transcendentals=KV * HALF * CTX
            ),
        )(lengths, q, keys, turned)

    other = attend(q_other)
    partner = lax.ppermute(other, "ctx", swap)
    own = attend(q_own)
    sent = call(pair_body, shape((CHIPS, MSG, DH), jnp.int16), [VMEM] * 2)(own, partner)
    got = lax.all_to_all(sent, "ctx", 0, 0, tiled=True, axis_index_groups=same_core)
    sent = call(merge_body, shape((parts, MSG, DH), bf16), [VMEM])(got)
    got = lax.all_to_all(sent, "head", 0, 0, tiled=True)
    heads = parts * KV * GRP
    return call(finish_body, (shape((TOK, heads * DH), bf16), shape((TOK, heads), f32)), [VMEM])(
        got
    )


def solution(mesh):
    return jax.shard_map(
        on_device,
        mesh=mesh,
        in_specs=(P("ctx", "head"), P("ctx", "head"), P("ctx", "head"), P("ctx")),
        out_specs=(P("ctx", None), P("ctx", None)),
        check_vma=False,
    )
```
